32 devices in a mesh: segment: 2 (over y), fsdp: 4 (over x, core), seq: 4 (over z).
Axes of the slice: x: 2, y: 2, z: 4, core: 2. Of those that a mesh axis runs over, the one named last changes fastest.
Arguments:
- arriving: bfloat16 [2, 4, 768, 2048], P('segment', 'fsdp', 'seq'), may hold values from -6 to 6
- gain: float32 [2, 2048], P('segment'), may hold values from 0.1 to 1.9
- input_weight: bfloat16 [2, 2048, 16, 3, 128], P('segment', 'fsdp', 'seq')
- output_weight: bfloat16 [2, 16, 128, 2048], P('segment', 'seq', None, 'fsdp'), may hold values from -1 to 1
- block_pattern: int32 [2, 4, 24, 6], P('segment', 'fsdp'), may hold values from 0 to 23, as said below
Outputs:
- passed: bfloat16 [2, 4, 768, 2048], P('segment', 'fsdp', 'seq')
The draws below stay inside these ranges and needn't reach their ends.
Inputs may be any that keep to these rules, and one draw needn't show every extreme that they name: `block_pattern`: row j of a document lists 6 different blocks; the first three are j - 1, j and j + 1 modulo 24, and block 0 is listed in every row.
All inputs are finite; a program needn't handle non-finite values.
Results may differ from the reference program's by a relative error of at most 0.012.
Values may be sent and summed in bfloat16 or wider, within the bound.
A program may use at most 64 MiB of HBM per device.

```python
import jax
import jax.numpy as jnp
from jax import lax

D = 2048
HEADS = 16
HEAD = 128
BLOCK = 32
SEL = 6
SEGMENTS = 2
DOCS = 4
LENGTH = 768
NBLOCKS = 24
N_SEQ = 4


def draw_input_weight(key, part):
    first_key = jax.random.fold_in(key, 0)
    matrix = jax.random.normal(first_key, (SEGMENTS, D, HEADS, 3, HEAD), jnp.float32) * D ** (-0.5)
    return matrix.astype(jnp.bfloat16)


def draw_block_pattern(key, part):
    block_ids = jnp.arange(NBLOCKS, dtype=jnp.int32)
    window_ids = jnp.stack([(block_ids - 1) % NBLOCKS, block_ids, (block_ids + 1) % NBLOCKS], axis=1)
    in_window = jnp.any(window_ids[:, :, None] == block_ids[None, None, :], axis=1)
    raw_scores = jax.random.randint(key, (SEGMENTS, DOCS, NBLOCKS, NBLOCKS), 0, 1 << 20, dtype=jnp.int32)
    ranked = raw_scores * NBLOCKS + block_ids
    ranked = jnp.where(block_ids == 0, 1 << 30, ranked)
    ranked = jnp.where(in_window, -1, ranked)
    ignored, picked = lax.top_k(ranked, SEL - 3)
    window_all = jnp.broadcast_to(window_ids, (SEGMENTS, DOCS, NBLOCKS, 3))
    return jnp.concatenate([window_all, picked.astype(jnp.int32)], axis=-1)


def steps_of(stream_key, shape, cuts, least, largest):
    level, own = 1.0, jax.random.fold_in(stream_key, 6)
    for position, parts in cuts:
        heights = jnp.exp(jax.random.uniform(jax.random.fold_in(own, position), (parts,), jnp.float32, least / len(cuts), largest / len(cuts)))
        level = level * jnp.repeat(heights, shape[position] // parts).reshape([-1 if axis == position else 1 for axis in range(len(shape))])
    return level


def normal_values(stream_key, extent, scale, reach, cuts=(), held_as=jnp.bfloat16):
    result = jax.random.normal(stream_key, extent, jnp.float32) * scale
    if len(cuts) > 0:
        result = steps_of(stream_key, extent, cuts, -0.22, 0.18) * result
    return jnp.clip(result, min=-reach, max=reach).astype(held_as)


def setup_inputs(seed: int = 0) -> dict:
    seeds = jax.random.split(jax.random.key(seed), 6)
    arriving = normal_values(seeds[0], (SEGMENTS, DOCS, LENGTH, D), 1.0, 6.0, ((0, 2), (1, 4), (2, 4)))
    gain = jnp.clip(1.0 + 0.18 * jax.random.normal(seeds[1], (SEGMENTS, D), jnp.float32), 0.1, 1.9)
    input_weight = draw_input_weight(jax.random.fold_in(seeds[5], 71), 0)
    output_weight = normal_values(seeds[3], (SEGMENTS, HEADS, HEAD, D), (HEAD // 4) ** -0.5, 1.0, ((0, 2), (1, 4), (3, 4)))
    block_pattern = draw_block_pattern(jax.random.fold_in(seeds[5], 71), 0)
    return {"arriving": arriving, "gain": gain, "input_weight": input_weight, "output_weight": output_weight, "block_pattern": block_pattern}


EPSILON = 1e-05

def normalize(tokens, gain_row):
    values = tokens.astype(jnp.float32)
    spread = lax.optimization_barrier(jnp.mean(values * values, axis=-1, keepdims=True))
    return (values * lax.rsqrt(spread + EPSILON) * gain_row).astype(jnp.bfloat16)

def one_document(tokens, gain_row, in_panel, out_panel, pattern_rows):
    normed = normalize(tokens, gain_row)
    projected = jnp.dot(normed, in_panel.reshape(D, HEADS * 3 * HEAD), preferred_element_type=jnp.float32)
    projected = projected.astype(jnp.bfloat16).reshape(LENGTH, HEADS, 3, HEAD)
    block_count = LENGTH // BLOCK
    query_rows = projected[:, :, 0].reshape(block_count, BLOCK, HEADS, HEAD).astype(jnp.float32)
    key_blocks = projected[:, :, 1].reshape(block_count, BLOCK, HEADS, HEAD)
    value_blocks = projected[:, :, 2].reshape(block_count, BLOCK, HEADS, HEAD)
    key_rows = key_blocks[pattern_rows].reshape(block_count, SEL * BLOCK, HEADS, HEAD).astype(jnp.float32)
    value_rows = value_blocks[pattern_rows].reshape(block_count, SEL * BLOCK, HEADS, HEAD).astype(jnp.float32)
    scores = jnp.einsum('qbhe,qnhe->hqbn', query_rows, key_rows, precision=lax.Precision.HIGHEST) * HEAD ** (-0.5)
    row_max = lax.optimization_barrier(jnp.max(scores, axis=-1, keepdims=True))
    exponent = jnp.exp(scores - row_max)
    weights = (exponent / lax.optimization_barrier(jnp.sum(exponent, axis=-1, keepdims=True))).astype(jnp.bfloat16)
    mixed_rows = jnp.einsum('hqbn,qnhe->qbhe', weights.astype(jnp.float32), value_rows, precision=lax.Precision.HIGHEST)
    mixed_rows = mixed_rows.astype(jnp.bfloat16).reshape(LENGTH, N_SEQ, HEADS // N_SEQ * HEAD).astype(jnp.float32)
    stacked = out_panel.reshape(N_SEQ, HEADS // N_SEQ * HEAD, D).astype(jnp.float32)
    partial_out = jnp.einsum('tgk,gkd->tgd', mixed_rows, stacked, precision=lax.Precision.HIGHEST)
    rounded = lax.optimization_barrier(partial_out.astype(jnp.bfloat16))
    branch = lax.optimization_barrier(jnp.sum(rounded.astype(jnp.float32), axis=1))
    return (tokens.astype(jnp.float32) + branch).astype(jnp.bfloat16)

def reference(arriving, gain, input_weight, output_weight, block_pattern):

    def one_segment(items):
        segment_tokens, gain_row, in_panel, out_panel, segment_pattern = items

        def one_item(doc_items):
            return one_document(doc_items[0], gain_row, in_panel, out_panel, doc_items[1])
        return lax.map(one_item, (segment_tokens, segment_pattern))
    updated = lax.map(one_segment, (arriving, gain, input_weight, output_weight, block_pattern))
    return jnp.roll(updated, 1, axis=0)
```

```python
import functools

import jax
import jax.numpy as jnp
from jax import lax
from jax.experimental import pallas as pl
from jax.experimental.pallas import tpu as pltpu
from jax.sharding import PartitionSpec as P

BLOCK = 32
SEL = 6
PIECE = 32
EPSILON = 1e-05
MESH = pl.DeviceIdType.MESH


def kernel(
    S, F, Z, HG,
    x_ref, gain_ref, w_ref, o_ref, pat_ref, out_ref,
    tok, win, wout, qkv, bias, in_l, in_r, outb, mixed, fin, acc,
    local_sem, zs, zr, ws, wr, vs, vr, rs, rr, ys, yr,
):
    rows, depth = x_ref.shape
    length = rows * Z
    slab, columns = w_ref.shape
    head = columns // (3 * HG)
    width = o_ref.shape[1]
    pieces = rows // PIECE
    half = slab // 2
    X = F // 2
    f32 = jnp.float32

    s = lax.axis_index("segment")
    f = lax.axis_index("fsdp")
    p = lax.axis_index("seq")
    core = lax.rem(f, 2)
    chip = lax.div(f, 2)
    sibling = f + 1 - 2 * core
    up = lax.rem(s + 1, S)
    down = lax.rem(s + S - 1, S)

    own_w = pltpu.make_async_copy(
        w_ref, win.at[pl.ds(pl.multiple_of(f * slab, slab), slab), :], local_sem.at[0])
    own_o = pltpu.make_async_copy(o_ref, wout.at[f], local_sem.at[1])
    own_w.start()
    own_o.start()

    barrier = pltpu.get_barrier_semaphore()

    def greet(device):
        pl.semaphore_signal(barrier, inc=1, device_id=device, device_id_type=MESH)

    pl.when(p > 0)(lambda: greet({"seq": p - 1}))
    pl.when(p < Z - 1)(lambda: greet({"seq": p + 1}))
    greet({"fsdp": sibling})
    for d in range(1, X):
        greet({"fsdp": lax.rem(chip + d, X) * 2 + core})
    greet({"segment": up})
    if S > 2:
        greet({"segment": down})
    always = 1 + (X - 1) + (2 if S > 2 else 1)
    pl.semaphore_wait(barrier, always + jnp.where(p > 0, 1, 0) + jnp.where(p < Z - 1, 1, 0))

    def w_rows(g, k):
        return win.at[pl.ds(pl.multiple_of(g * slab + k * half, half), half), :]

    def w_copy(g, k, device, slot, own):
        src = w_ref.at[pl.ds(k * half, half), :] if own else w_rows(g, k)
        return pltpu.make_async_remote_copy(
            src_ref=src, dst_ref=w_rows(g, k), send_sem=ws.at[slot, k], recv_sem=wr.at[g, k],
            device_id={"fsdp": device}, device_id_type=MESH)

    def o_copy(g, device, slot, own):
        src = o_ref if own else wout.at[g]
        return pltpu.make_async_remote_copy(
            src_ref=src, dst_ref=wout.at[g], send_sem=vs.at[slot], recv_sem=vr.at[g],
            device_id={"fsdp": device}, device_id_type=MESH)

    def peer(d):
        return lax.rem(chip + d, X) * 2 + core

    def source(d):
        return lax.rem(chip + X - d, X) * 2 + core

    for k in range(2):
        for d in range(1, X):
            w_copy(f, k, peer(d), d - 1, True).start()
        w_copy(f, k, sibling, X - 1, True).start()

    def t_rows(c, j):
        return tok.at[pl.ds(pl.multiple_of(c * rows + j * PIECE, PIECE), PIECE), :]

    def t_copy(c, j, direction, step):
        device = p + 1 if direction == 0 else p - 1
        return pltpu.make_async_remote_copy(
            src_ref=t_rows(c, j), dst_ref=t_rows(c, j),
            send_sem=zs.at[direction, step, j], recv_sem=zr.at[direction, step, j],
            device_id={"seq": device}, device_id_type=MESH)

    def norm_piece(j, carry):
        values = x_ref[pl.ds(pl.multiple_of(j * PIECE, PIECE), PIECE), :].astype(f32)
        spread = jnp.mean(values * values, axis=-1, keepdims=True)
        t_rows(p, j)[...] = (values * lax.rsqrt(spread + EPSILON) * gain_ref[...]).astype(jnp.bfloat16)
        pl.when(p < Z - 1)(lambda: t_copy(p, j, 0, 0).start())
        pl.when(p > 0)(lambda: t_copy(p, j, 1, 0).start())
        return carry

    lax.fori_loop(0, pieces, norm_piece, 0)

    key_block = lax.broadcasted_iota(jnp.int32, (BLOCK, length), 1) // BLOCK

    def bias_rows(b, carry):
        hit = key_block == pat_ref[b, 0]
        for i in range(1, SEL):
            hit = jnp.logical_or(hit, key_block == pat_ref[b, i])
        bias[pl.ds(pl.multiple_of(b * BLOCK, BLOCK), BLOCK), :] = jnp.where(hit, 0.0, -1e30)
        return carry

    lax.fori_loop(0, length // BLOCK, bias_rows, 0)

    def receive(t, forward):
        def one(j, carry):
            @pl.when(t < p)
            def _():
                t_copy(p - 1 - t, j, 0, t).wait_recv()
                if forward:
                    pl.when(p < Z - 1)(lambda: t_copy(p - 1 - t, j, 0, t + 1).start())

            @pl.when(t < Z - 1 - p)
            def _():
                t_copy(p + 1 + t, j, 1, t).wait_recv()
                if forward:
                    pl.when(p > 0)(lambda: t_copy(p + 1 + t, j, 1, t + 1).start())
            return carry

        lax.fori_loop(0, pieces, one, 0)

    def forward_w(k):
        for d in range(1, X):
            w_copy(source(d), k, sibling, X - 1 + d, False).wait_recv()
            w_copy(source(d), k, sibling, X - 1 + d, False).start()

    for t in range(Z - 2):
        receive(t, True)
        if t < 2:
            forward_w(t)
    for k in range(min(2, Z - 2), 2):
        forward_w(k)
    for d in range(1, X):
        o_copy(f, peer(d), d - 1, True).start()
    o_copy(f, sibling, X - 1, True).start()
    own_w.wait()
    for k in range(2):
        for d in range(X):
            other = lax.rem(chip + d, X) * 2 + 1 - core
            w_copy(other, k, sibling, 0, False).wait_recv()

    def project(e, carry):
        d = lax.div(e, 2)
        side = lax.rem(e, 2)

        @pl.when(e == 2 * Z - 2)
        def _():
            receive(Z - 2, False)
        c = jnp.where(side == 0, p - d, p + d)
        valid = jnp.where(side == 0, d <= p, jnp.logical_and(d >= 1, d <= Z - 1 - p))

        @pl.when(valid)
        def _():
            at = pl.ds(pl.multiple_of(c * rows, rows), rows)

            def one(h, inner):
                cols = pl.ds(pl.multiple_of(h * 3 * head, 3 * head), 3 * head)
                qkv[at, cols] = jnp.dot(
                    tok[at, :], win[:, cols], preferred_element_type=f32).astype(jnp.bfloat16)
                return inner

            lax.fori_loop(0, HG, one, 0)
        return carry

    lax.fori_loop(0, 2 * Z, project, 0)

    for d in range(1, X):
        o_copy(source(d), sibling, X - 1 + d, False).wait_recv()
        o_copy(source(d), sibling, X - 1 + d, False).start()
    own_o.wait()
    for d in range(X):
        o_copy(lax.rem(chip + d, X) * 2 + 1 - core, sibling, 0, False).wait_recv()

    def partial(c):
        at = pl.ds(pl.multiple_of(c * rows, rows), rows)
        for h in range(HG):
            base = h * 3 * head
            q = qkv[at, base:base + head]
            k = qkv[:, base + head:base + 2 * head]
            v = qkv[:, base + 2 * head:base + 3 * head]
            scores = lax.dot_general(q, k, (((1,), (1,)), ((), ())), preferred_element_type=f32)
            scores = scores * head ** (-0.5) + bias[at, :]
            exponent = jnp.exp(scores - jnp.max(scores, axis=-1, keepdims=True))
            total = jnp.sum(exponent, axis=-1, keepdims=True)
            value = jnp.dot(exponent.astype(jnp.bfloat16), v, preferred_element_type=f32)
            mixed[:, h * head:(h + 1) * head] = (value / total).astype(jnp.bfloat16)
        for g in range(F):
            outb[c, :, g * width:(g + 1) * width] = jnp.dot(
                mixed[...], wout[g], preferred_element_type=f32).astype(jnp.bfloat16)

    def s_copy(c, j, direction):
        device = p + 1 if direction == 0 else p - 1
        inbox = in_l if direction == 0 else in_r
        at = pl.ds(pl.multiple_of(j * PIECE, PIECE), PIECE)
        return pltpu.make_async_remote_copy(
            src_ref=outb.at[c, at, :], dst_ref=inbox.at[c, at, :],
            send_sem=rs.at[direction, c, j], recv_sem=rr.at[direction, c, j],
            device_id={"seq": device}, device_id_type=MESH)

    def y_copy(j):
        at = pl.ds(pl.multiple_of(j * PIECE, PIECE), PIECE)
        return pltpu.make_async_remote_copy(
            src_ref=fin.at[at, :], dst_ref=out_ref.at[at, :], send_sem=ys.at[j], recv_sem=yr.at[j],
            device_id={"segment": up}, device_id_type=MESH)

    def add_in(c, j, inbox):
        at = pl.ds(pl.multiple_of(j * PIECE, PIECE), PIECE)
        outb[c, at, :] = (outb[c, at, :].astype(f32) + inbox[c, at, :].astype(f32)).astype(jnp.bfloat16)

    def reduce_step(u, carry):
        own = u == Z - 1
        right = Z - 1 - u
        goes_right = jnp.logical_and(jnp.logical_not(own), right > p)
        goes_left = jnp.logical_and(jnp.logical_not(own), u < p)

        def side_of(side, inner):
            c = jnp.where(side == 0, jnp.where(own, p, right), u)
            valid = jnp.where(side == 0, jnp.logical_or(own, goes_right), goes_left)
            pl.when(valid)(lambda: partial(c))
            return inner

        lax.fori_loop(0, 2, side_of, 0)

        def one(j, inner):
            @pl.when(goes_right)
            def _():
                @pl.when(p > 0)
                def _():
                    s_copy(right, j, 0).wait_recv()
                    add_in(right, j, in_l)
                s_copy(right, j, 0).start()

            @pl.when(goes_left)
            def _():
                @pl.when(p < Z - 1)
                def _():
                    s_copy(u, j, 1).wait_recv()
                    add_in(u, j, in_r)
                s_copy(u, j, 1).start()
            return inner

        lax.fori_loop(0, pieces, one, 0)
        return carry

    lax.fori_loop(0, Z, reduce_step, 0)

    def finish(j, carry):
        at = pl.ds(pl.multiple_of(j * PIECE, PIECE), PIECE)
        acc[...] = outb[p, at, :].astype(f32)

        @pl.when(p < Z - 1)
        def _():
            s_copy(p, j, 1).wait_recv()
            acc[...] += in_r[p, at, :].astype(f32)

        @pl.when(p > 0)
        def _():
            s_copy(p, j, 0).wait_recv()
            acc[...] += in_l[p, at, :].astype(f32)
        fin[at, :] = (x_ref[at, :].astype(f32) + acc[...]).astype(jnp.bfloat16)
        y_copy(j).start()
        return carry

    lax.fori_loop(0, pieces, finish, 0)

    for k in range(2):
        for slot in range(2 * X - 1):
            w_copy(f, k, sibling, slot, False).wait_send()
    for slot in range(2 * X - 1):
        o_copy(f, sibling, slot, False).wait_send()

    def sent(j, carry):
        for t in range(Z - 1):
            @pl.when(jnp.logical_and(p < Z - 1, t <= p))
            def _():
                t_copy(p, j, 0, t).wait_send()

            @pl.when(jnp.logical_and(p > 0, t <= Z - 1 - p))
            def _():
                t_copy(p, j, 1, t).wait_send()
        for c in range(Z):
            pl.when(c > p)(lambda: s_copy(c, j, 0).wait_send())
            pl.when(c < p)(lambda: s_copy(c, j, 1).wait_send())
        y_copy(j).wait_send()
        y_copy(j).wait_recv()
        return carry

    lax.fori_loop(0, pieces, sent, 0)


def body(arriving, gain, input_weight, output_weight, block_pattern, S, F, Z):
    tokens = arriving[0, 0]
    rows, depth = tokens.shape
    slab, HG, triple, head = input_weight.shape[1:]
    columns = HG * triple * head
    width = output_weight.shape[-1]
    length = rows * Z
    pieces = rows // PIECE
    X = F // 2
    bf16 = jnp.bfloat16
    dma = pltpu.SemaphoreType.DMA
    vmem = pl.BlockSpec(memory_space=pltpu.VMEM)
    anywhere = pl.BlockSpec(memory_space=pl.ANY)
    passed = pl.pallas_call(
        functools.partial(kernel, S, F, Z, HG),
        out_shape=jax.ShapeDtypeStruct((rows, depth), bf16),
        in_specs=[vmem, vmem, anywhere, anywhere, pl.BlockSpec(memory_space=pltpu.SMEM)],
        out_specs=anywhere,
        scratch_shapes=[
            pltpu.VMEM((length, depth), bf16),
            pltpu.VMEM((depth, columns), bf16),
            pltpu.VMEM((F, HG * head, width), bf16),
            pltpu.VMEM((length, columns), bf16),
            pltpu.VMEM((length, length), jnp.float32),
            pltpu.VMEM((Z, rows, depth), bf16),
            pltpu.VMEM((Z, rows, depth), bf16),
            pltpu.VMEM((Z, rows, depth), bf16),
            pltpu.VMEM((rows, HG * head), bf16),
            pltpu.VMEM((rows, depth), bf16),
            pltpu.VMEM((PIECE, depth), jnp.float32),
            dma((2,)),
            dma((2, Z - 1, pieces)),
            dma((2, Z - 1, pieces)),
            dma((2 * X - 1, 2)),
            dma((F, 2)),
            dma((2 * X - 1,)),
            dma((F,)),
            dma((2, Z, pieces)),
            dma((2, Z, pieces)),
            dma((pieces,)),
            dma((pieces,)),
        ],
        compiler_params=pltpu.CompilerParams(
            collective_id=0, has_side_effects=True, vmem_limit_bytes=48 * 1024 * 1024
        ),
    )(
        tokens,
        gain,
        input_weight[0].reshape(slab, columns),
        output_weight[0].reshape(HG * head, width),
        block_pattern[0, 0],
    )
    return passed[None, None]


def solution(mesh):
    in_specs = (
        P("segment", "fsdp", "seq", None),
        P("segment", None),
        P("segment", "fsdp", "seq", None, None),
        P("segment", "seq", None, "fsdp"),
        P("segment", "fsdp", None, None),
    )
    out_specs = P("segment", "fsdp", "seq", None)
    sizes = {"S": mesh.shape["segment"], "F": mesh.shape["fsdp"], "Z": mesh.shape["seq"]}
    return jax.shard_map(
        functools.partial(body, **sizes), mesh=mesh, in_specs=in_specs, out_specs=out_specs, check_vma=False
    )
```

```python
import functools

import jax
import jax.numpy as jnp
from jax import lax
from jax.experimental import pallas as pl
from jax.experimental.pallas import tpu as pltpu
from jax.sharding import PartitionSpec as P

BLOCK = 32
SEL = 6
PIECE = 32
EPSILON = 1e-05
MESH = pl.DeviceIdType.MESH


def kernel(
    S, F, Z, HG,
    x_ref, gain_ref, w_ref, o_ref, pat_ref, out_ref,
    tok, win, wout, qkv, bias, in_l, in_r, outb, mixed, fin, acc,
    local_sem, zs, zr, ws, wr, vs, vr, rs, rr, ys, yr,
):
    rows, depth = x_ref.shape
    length = rows * Z
    slab, columns = w_ref.shape
    head = columns // (3 * HG)
    width = o_ref.shape[1]
    pieces = rows // PIECE
    half = slab // 2
    X = F // 2
    f32 = jnp.float32

    s = lax.axis_index("segment")
    f = lax.axis_index("fsdp")
    p = lax.axis_index("seq")
    core = lax.rem(f, 2)
    chip = lax.div(f, 2)
    sibling = f + 1 - 2 * core
    up = lax.rem(s + 1, S)
    down = lax.rem(s + S - 1, S)

    own_w = pltpu.make_async_copy(
        w_ref, win.at[pl.ds(pl.multiple_of(f * slab, slab), slab), :], local_sem.at[0])
    own_o = pltpu.make_async_copy(o_ref, wout.at[f], local_sem.at[1])
    own_w.start()
    own_o.start()

    barrier = pltpu.get_barrier_semaphore()

    def greet(device):
        pl.semaphore_signal(barrier, inc=1, device_id=device, device_id_type=MESH)

    pl.when(p > 0)(lambda: greet({"seq": p - 1}))
    pl.when(p < Z - 1)(lambda: greet({"seq": p + 1}))
    greet({"fsdp": sibling})
    for d in range(1, X):
        greet({"fsdp": lax.rem(chip + d, X) * 2 + core})
    greet({"segment": up})
    if S > 2:
        greet({"segment": down})
    always = 1 + (X - 1) + (2 if S > 2 else 1)
    pl.semaphore_wait(barrier, always + jnp.where(p > 0, 1, 0) + jnp.where(p < Z - 1, 1, 0))

    def w_rows(g, k):
        return win.at[pl.ds(pl.multiple_of(g * slab + k * half, half), half), :]

    def w_copy(g, k, device, slot, own):
        src = w_ref.at[pl.ds(k * half, half), :] if own else w_rows(g, k)
        return pltpu.make_async_remote_copy(
            src_ref=src, dst_ref=w_rows(g, k), send_sem=ws.at[slot, k], recv_sem=wr.at[g, k],
            device_id={"fsdp": device}, device_id_type=MESH)

    def o_copy(g, device, slot, own):
        src = o_ref if own else wout.at[g]
        return pltpu.make_async_remote_copy(
            src_ref=src, dst_ref=wout.at[g], send_sem=vs.at[slot], recv_sem=vr.at[g],
            device_id={"fsdp": device}, device_id_type=MESH)

    def peer(d):
        return lax.rem(chip + d, X) * 2 + core

    def source(d):
        return lax.rem(chip + X - d, X) * 2 + core

    for k in range(2):
        for d in range(1, X):
            w_copy(f, k, peer(d), d - 1, True).start()
        w_copy(f, k, sibling, X - 1, True).start()

    def t_rows(c, j):
        return tok.at[pl.ds(pl.multiple_of(c * rows + j * PIECE, PIECE), PIECE), :]

    def t_copy(c, j, direction, step):
        device = p + 1 if direction == 0 else p - 1
        return pltpu.make_async_remote_copy(
            src_ref=t_rows(c, j), dst_ref=t_rows(c, j),
            send_sem=zs.at[direction, step, j], recv_sem=zr.at[direction, step, j],
            device_id={"seq": device}, device_id_type=MESH)

    def norm_piece(j, carry):
        values = x_ref[pl.ds(pl.multiple_of(j * PIECE, PIECE), PIECE), :].astype(f32)
        spread = jnp.mean(values * values, axis=-1, keepdims=True)
        t_rows(p, j)[...] = (values * lax.rsqrt(spread + EPSILON) * gain_ref[...]).astype(jnp.bfloat16)
        pl.when(p < Z - 1)(lambda: t_copy(p, j, 0, 0).start())
        pl.when(p > 0)(lambda: t_copy(p, j, 1, 0).start())
        return carry

    lax.fori_loop(0, pieces, norm_piece, 0)

    key_block = lax.broadcasted_iota(jnp.int32, (BLOCK, length), 1) // BLOCK

    def bias_rows(b, carry):
        hit = key_block == pat_ref[b, 0]
        for i in range(1, SEL):
            hit = jnp.logical_or(hit, key_block == pat_ref[b, i])
        bias[pl.ds(pl.multiple_of(b * BLOCK, BLOCK), BLOCK), :] = jnp.where(hit, 0.0, -1e30)
        return carry

    lax.fori_loop(0, length // BLOCK, bias_rows, 0)

    def receive(t, forward):
        def one(j, carry):
            @pl.when(t < p)
            def _():
                t_copy(p - 1 - t, j, 0, t).wait_recv()
                if forward:
                    pl.when(p < Z - 1)(lambda: t_copy(p - 1 - t, j, 0, t + 1).start())

            @pl.when(t < Z - 1 - p)
            def _():
                t_copy(p + 1 + t, j, 1, t).wait_recv()
                if forward:
                    pl.when(p > 0)(lambda: t_copy(p + 1 + t, j, 1, t + 1).start())
            return carry

        lax.fori_loop(0, pieces, one, 0)

    def forward_w(k):
        for d in range(1, X):
            w_copy(source(d), k, sibling, X - 1 + d, False).wait_recv()
            w_copy(source(d), k, sibling, X - 1 + d, False).start()

    for t in range(Z - 2):
        receive(t, True)
        if t < 2:
            forward_w(t)
    for k in range(min(2, Z - 2), 2):
        forward_w(k)
    for d in range(1, X):
        o_copy(f, peer(d), d - 1, True).start()
    o_copy(f, sibling, X - 1, True).start()
    own_w.wait()
    for k in range(2):
        for d in range(X):
            other = lax.rem(chip + d, X) * 2 + 1 - core
            w_copy(other, k, sibling, 0, False).wait_recv()

    def project(e, carry):
        d = lax.div(e, 2)
        side = lax.rem(e, 2)

        @pl.when(e == 2 * Z - 2)
        def _():
            receive(Z - 2, False)
        c = jnp.where(side == 0, p - d, p + d)
        valid = jnp.where(side == 0, d <= p, jnp.logical_and(d >= 1, d <= Z - 1 - p))

        @pl.when(valid)
        def _():
            at = pl.ds(pl.multiple_of(c * rows, rows), rows)

            def one(h, inner):
                cols = pl.ds(pl.multiple_of(h * 3 * head, 3 * head), 3 * head)
                qkv[at, cols] = jnp.dot(
                    tok[at, :], win[:, cols], preferred_element_type=f32).astype(jnp.bfloat16)
                return inner

            lax.fori_loop(0, HG, one, 0)
        return carry

    lax.fori_loop(0, 2 * Z, project, 0)

    for d in range(1, X):
        o_copy(source(d), sibling, X - 1 + d, False).wait_recv()
        o_copy(source(d), sibling, X - 1 + d, False).start()
    own_o.wait()
    for d in range(X):
        o_copy(lax.rem(chip + d, X) * 2 + 1 - core, sibling, 0, False).wait_recv()

    def partial(c):
        at = pl.ds(pl.multiple_of(c * rows, rows), rows)
        for h in range(HG):
            base = h * 3 * head
            q = qkv[at, base:base + head]
            k = qkv[:, base + head:base + 2 * head]
            v = qkv[:, base + 2 * head:base + 3 * head]
            scores = lax.dot_general(q, k, (((1,), (1,)), ((), ())), preferred_element_type=f32)
            scores = scores * head ** (-0.5) + bias[at, :]
            exponent = jnp.exp(scores - jnp.max(scores, axis=-1, keepdims=True))
            total = jnp.sum(exponent, axis=-1, keepdims=True)
            value = jnp.dot(exponent.astype(jnp.bfloat16), v, preferred_element_type=f32)
            mixed[:, h * head:(h + 1) * head] = (value / total).astype(jnp.bfloat16)
        for g in range(F):
            outb[c, :, g * width:(g + 1) * width] = jnp.dot(
                mixed[...], wout[g], preferred_element_type=f32).astype(jnp.bfloat16)

    def s_copy(c, j, direction):
        device = p + 1 if direction == 0 else p - 1
        inbox = in_l if direction == 0 else in_r
        at = pl.ds(pl.multiple_of(j * PIECE, PIECE), PIECE)
        return pltpu.make_async_remote_copy(
            src_ref=outb.at[c, at, :], dst_ref=inbox.at[c, at, :],
            send_sem=rs.at[direction, c, j], recv_sem=rr.at[direction, c, j],
            device_id={"seq": device}, device_id_type=MESH)

    def y_copy(j):
        at = pl.ds(pl.multiple_of(j * PIECE, PIECE), PIECE)
        return pltpu.make_async_remote_copy(
            src_ref=fin.at[at, :], dst_ref=out_ref.at[at, :], send_sem=ys.at[j], recv_sem=yr.at[j],
            device_id={"segment": up}, device_id_type=MESH)

    def add_in(c, j, inbox):
        at = pl.ds(pl.multiple_of(j * PIECE, PIECE), PIECE)
        outb[c, at, :] = (outb[c, at, :].astype(f32) + inbox[c, at, :].astype(f32)).astype(jnp.bfloat16)

    def send_all(c, direction):
        def one(j, inner):
            s_copy(c, j, direction).start()
            return inner

        lax.fori_loop(0, pieces, one, 0)

    def share(e, carry):
        u = lax.div(e, 2)
        side = lax.rem(e, 2)
        own = u == Z - 1
        right = Z - 1 - u
        c = jnp.where(side == 0, jnp.where(own, p, right), u)
        valid = jnp.where(side == 0, jnp.logical_or(own, right > p), jnp.logical_and(jnp.logical_not(own), u < p))
        pl.when(valid)(lambda: partial(c))
        leaves = jnp.logical_and(valid, jnp.logical_not(own))
        pl.when(jnp.logical_and(leaves, jnp.logical_and(side == 0, p == 0)))(lambda: send_all(c, 0))
        pl.when(jnp.logical_and(leaves, jnp.logical_and(side == 1, p == Z - 1)))(lambda: send_all(c, 1))
        return carry

    lax.fori_loop(0, 2 * Z, share, 0)

    def relay(step, carry):
        r = step - p
        l = step - (Z - 1 - p)

        @pl.when(jnp.logical_and(p > 0, jnp.logical_and(r >= 0, r < (Z - 1 - p) * pieces)))
        def _():
            c, j = Z - 1 - lax.div(r, pieces), lax.rem(r, pieces)
            s_copy(c, j, 0).wait_recv()
            add_in(c, j, in_l)
            s_copy(c, j, 0).start()

        @pl.when(jnp.logical_and(p < Z - 1, jnp.logical_and(l >= 0, l < p * pieces)))
        def _():
            c, j = lax.div(l, pieces), lax.rem(l, pieces)
            s_copy(c, j, 1).wait_recv()
            add_in(c, j, in_r)
            s_copy(c, j, 1).start()
        return carry

    lax.fori_loop(0, (Z - 1) * pieces + Z, relay, 0)

    def finish(j, carry):
        at = pl.ds(pl.multiple_of(j * PIECE, PIECE), PIECE)
        acc[...] = outb[p, at, :].astype(f32)

        @pl.when(p < Z - 1)
        def _():
            s_copy(p, j, 1).wait_recv()
            acc[...] += in_r[p, at, :].astype(f32)

        @pl.when(p > 0)
        def _():
            s_copy(p, j, 0).wait_recv()
            acc[...] += in_l[p, at, :].astype(f32)
        fin[at, :] = (x_ref[at, :].astype(f32) + acc[...]).astype(jnp.bfloat16)
        y_copy(j).start()
        return carry

    lax.fori_loop(0, pieces, finish, 0)

    for k in range(2):
        for slot in range(2 * X - 1):
            w_copy(f, k, sibling, slot, False).wait_send()
    for slot in range(2 * X - 1):
        o_copy(f, sibling, slot, False).wait_send()

    def sent(j, carry):
        for t in range(Z - 1):
            @pl.when(jnp.logical_and(p < Z - 1, t <= p))
            def _():
                t_copy(p, j, 0, t).wait_send()

            @pl.when(jnp.logical_and(p > 0, t <= Z - 1 - p))
            def _():
                t_copy(p, j, 1, t).wait_send()
        for c in range(Z):
            pl.when(c > p)(lambda: s_copy(c, j, 0).wait_send())
            pl.when(c < p)(lambda: s_copy(c, j, 1).wait_send())
        y_copy(j).wait_send()
        y_copy(j).wait_recv()
        return carry

    lax.fori_loop(0, pieces, sent, 0)


def body(arriving, gain, input_weight, output_weight, block_pattern, S, F, Z):
    tokens = arriving[0, 0]
    rows, depth = tokens.shape
    slab, HG, triple, head = input_weight.shape[1:]
    columns = HG * triple * head
    width = output_weight.shape[-1]
    length = rows * Z
    pieces = rows // PIECE
    X = F // 2
    bf16 = jnp.bfloat16
    dma = pltpu.SemaphoreType.DMA
    vmem = pl.BlockSpec(memory_space=pltpu.VMEM)
    anywhere = pl.BlockSpec(memory_space=pl.ANY)
    passed = pl.pallas_call(
        functools.partial(kernel, S, F, Z, HG),
        out_shape=jax.ShapeDtypeStruct((rows, depth), bf16),
        in_specs=[vmem, vmem, anywhere, anywhere, pl.BlockSpec(memory_space=pltpu.SMEM)],
        out_specs=anywhere,
        scratch_shapes=[
            pltpu.VMEM((length, depth), bf16),
            pltpu.VMEM((depth, columns), bf16),
            pltpu.VMEM((F, HG * head, width), bf16),
            pltpu.VMEM((length, columns), bf16),
            pltpu.VMEM((length, length), jnp.float32),
            pltpu.VMEM((Z, rows, depth), bf16),
            pltpu.VMEM((Z, rows, depth), bf16),
            pltpu.VMEM((Z, rows, depth), bf16),
            pltpu.VMEM((rows, HG * head), bf16),
            pltpu.VMEM((rows, depth), bf16),
            pltpu.VMEM((PIECE, depth), jnp.float32),
            dma((2,)),
            dma((2, Z - 1, pieces)),
            dma((2, Z - 1, pieces)),
            dma((2 * X - 1, 2)),
            dma((F, 2)),
            dma((2 * X - 1,)),
            dma((F,)),
            dma((2, Z, pieces)),
            dma((2, Z, pieces)),
            dma((pieces,)),
            dma((pieces,)),
        ],
        compiler_params=pltpu.CompilerParams(
            collective_id=0, has_side_effects=True, vmem_limit_bytes=48 * 1024 * 1024
        ),
    )(
        tokens,
        gain,
        input_weight[0].reshape(slab, columns),
        output_weight[0].reshape(HG * head, width),
        block_pattern[0, 0],
    )
    return passed[None, None]


def solution(mesh):
    in_specs = (
        P("segment", "fsdp", "seq", None),
        P("segment", None),
        P("segment", "fsdp", "seq", None, None),
        P("segment", "seq", None, "fsdp"),
        P("segment", "fsdp", None, None),
    )
    out_specs = P("segment", "fsdp", "seq", None)
    sizes = {"S": mesh.shape["segment"], "F": mesh.shape["fsdp"], "Z": mesh.shape["seq"]}
    return jax.shard_map(
        functools.partial(body, **sizes), mesh=mesh, in_specs=in_specs, out_specs=out_specs, check_vma=False
    )
```

```python
import functools

import jax
import jax.numpy as jnp
from jax import lax
from jax.experimental import pallas as pl
from jax.experimental.pallas import tpu as pltpu
from jax.sharding import PartitionSpec as P

BLOCK = 32
SEL = 6
PIECE = 32
STRIP = 32
PARTS = 4
EPSILON = 1e-05
MESH = pl.DeviceIdType.MESH


def kernel(
    S, F, Z, HG,
    x_ref, gain_ref, w_ref, o_ref, pat_ref, out_ref,
    raw, tok, win, wout, qkv, bias, in_l, in_r, outb, mixed, fin, acc,
    local_sem, zs, zr, ws, wr, vs, vr, rs, rr, ys, yr,
):
    rows, depth = x_ref.shape
    length = rows * Z
    slab, head = w_ref.shape[0], w_ref.shape[3]
    columns = 3 * HG * head
    width = o_ref.shape[1]
    pieces = rows // PIECE
    part = slab // PARTS
    half = o_ref.shape[0] // 2
    X = F // 2
    f32 = jnp.float32

    s = lax.axis_index("segment")
    f = lax.axis_index("fsdp")
    p = lax.axis_index("seq")
    core = lax.rem(f, 2)
    chip = lax.div(f, 2)
    sibling = f + 1 - 2 * core
    up = lax.rem(s + 1, S)
    down = lax.rem(s + S - 1, S)

    own_w = pltpu.make_async_copy(w_ref, raw, local_sem.at[0])
    own_o = pltpu.make_async_copy(o_ref, wout.at[f], local_sem.at[1])
    own_w.start()
    own_o.start()

    barrier = pltpu.get_barrier_semaphore()

    def greet(device):
        pl.semaphore_signal(barrier, inc=1, device_id=device, device_id_type=MESH)

    pl.when(p > 0)(lambda: greet({"seq": p - 1}))
    pl.when(p < Z - 1)(lambda: greet({"seq": p + 1}))
    greet({"fsdp": sibling})
    for d in range(1, X):
        greet({"fsdp": lax.rem(chip + d, X) * 2 + core})
    greet({"segment": up})
    if S > 2:
        greet({"segment": down})
    always = 1 + (X - 1) + (2 if S > 2 else 1)
    pl.semaphore_wait(barrier, always + jnp.where(p > 0, 1, 0) + jnp.where(p < Z - 1, 1, 0))

    def w_rows(g, k):
        return win.at[pl.ds(pl.multiple_of(g * slab + k * part, part), part), :]

    def w_copy(g, k, device, slot):
        return pltpu.make_async_remote_copy(
            src_ref=w_rows(g, k), dst_ref=w_rows(g, k), send_sem=ws.at[slot, k], recv_sem=wr.at[g, k],
            device_id={"fsdp": device}, device_id_type=MESH)

    def o_copy(g, k, device, slot, own=False):
        at = pl.ds(k * half, half)
        return pltpu.make_async_remote_copy(
            src_ref=o_ref.at[at, :] if own else wout.at[g, at, :], dst_ref=wout.at[g, at, :],
            send_sem=vs.at[slot, k], recv_sem=vr.at[g, k],
            device_id={"fsdp": device}, device_id_type=MESH)

    def peer(d):
        return lax.rem(chip + d, X) * 2 + core

    def source(d):
        return lax.rem(chip + X - d, X) * 2 + core

    def send_o(k):
        for d in range(1, X):
            o_copy(f, k, peer(d), d - 1, True).start()
        o_copy(f, k, sibling, X - 1, True).start()

    def forward_o(k):
        for d in range(1, X):
            o_copy(source(d), k, sibling, X - 1 + d).wait_recv()
            o_copy(source(d), k, sibling, X - 1 + d).start()

    send_o(0)

    def t_rows(c, j):
        return tok.at[pl.ds(pl.multiple_of(c * rows + j * PIECE, PIECE), PIECE), :]

    def t_copy(c, j, direction, step):
        device = p + 1 if direction == 0 else p - 1
        return pltpu.make_async_remote_copy(
            src_ref=t_rows(c, j), dst_ref=t_rows(c, j),
            send_sem=zs.at[direction, step, j], recv_sem=zr.at[direction, step, j],
            device_id={"seq": device}, device_id_type=MESH)

    def norm_piece(j, carry):
        values = x_ref[pl.ds(pl.multiple_of(j * PIECE, PIECE), PIECE), :].astype(f32)
        spread = jnp.mean(values * values, axis=-1, keepdims=True)
        t_rows(p, j)[...] = (values * lax.rsqrt(spread + EPSILON) * gain_ref[...]).astype(jnp.bfloat16)
        pl.when(p < Z - 1)(lambda: t_copy(p, j, 0, 0).start())
        pl.when(p > 0)(lambda: t_copy(p, j, 1, 0).start())
        return carry

    lax.fori_loop(0, pieces, norm_piece, 0)

    own_w.wait()

    def flatten(i, carry):
        flat = raw[pl.ds(i * STRIP, STRIP)].astype(f32).reshape(STRIP, columns)
        win[pl.ds(pl.multiple_of(f * slab + i * STRIP, STRIP), STRIP), :] = flat.astype(jnp.bfloat16)
        return carry

    for k in range(PARTS):
        lax.fori_loop(k * (part // STRIP), (k + 1) * (part // STRIP), flatten, 0)
        for d in range(1, X):
            w_copy(f, k, peer(d), d - 1).start()
        w_copy(f, k, sibling, X - 1).start()

    key_block = lax.broadcasted_iota(jnp.int32, (BLOCK, length), 1) // BLOCK

    def bias_rows(b, carry):
        hit = key_block == pat_ref[b, 0]
        for i in range(1, SEL):
            hit = jnp.logical_or(hit, key_block == pat_ref[b, i])
        bias[pl.ds(pl.multiple_of(b * BLOCK, BLOCK), BLOCK), :] = jnp.where(hit, 0.0, -1e30)
        return carry

    lax.fori_loop(0, length // BLOCK, bias_rows, 0)

    def receive(t, forward):
        def one(j, carry):
            @pl.when(t < p)
            def _():
                t_copy(p - 1 - t, j, 0, t).wait_recv()
                if forward:
                    pl.when(p < Z - 1)(lambda: t_copy(p - 1 - t, j, 0, t + 1).start())

            @pl.when(t < Z - 1 - p)
            def _():
                t_copy(p + 1 + t, j, 1, t).wait_recv()
                if forward:
                    pl.when(p > 0)(lambda: t_copy(p + 1 + t, j, 1, t + 1).start())
            return carry

        lax.fori_loop(0, pieces, one, 0)

    def forward_w(k):
        for d in range(1, X):
            w_copy(source(d), k, sibling, X - 1 + d).wait_recv()
            w_copy(source(d), k, sibling, X - 1 + d).start()

    share_of = -(-PARTS // (Z - 2))
    for t in range(Z - 2):
        receive(t, True)
        for k in range(t * share_of, min(PARTS, (t + 1) * share_of)):
            forward_w(k)
    send_o(1)
    forward_o(0)
    for k in range(PARTS):
        for d in range(X):
            w_copy(lax.rem(chip + d, X) * 2 + 1 - core, k, sibling, 0).wait_recv()

    def project(e, carry):
        d = lax.div(e, 2)
        side = lax.rem(e, 2)

        @pl.when(e == 2 * Z - 2)
        def _():
            receive(Z - 2, False)
        c = jnp.where(side == 0, p - d, p + d)
        valid = jnp.where(side == 0, d <= p, jnp.logical_and(d >= 1, d <= Z - 1 - p))

        @pl.when(valid)
        def _():
            at = pl.ds(pl.multiple_of(c * rows, rows), rows)

            def one(h, inner):
                cols = pl.ds(pl.multiple_of(h * 3 * head, 3 * head), 3 * head)
                qkv[at, cols] = jnp.dot(
                    tok[at, :], win[:, cols], preferred_element_type=f32).astype(jnp.bfloat16)
                return inner

            lax.fori_loop(0, HG, one, 0)
        return carry

    lax.fori_loop(0, 2 * Z, project, 0)

    forward_o(1)
    own_o.wait()
    for k in range(2):
        for d in range(X):
            o_copy(lax.rem(chip + d, X) * 2 + 1 - core, k, sibling, 0).wait_recv()

    def partial(c):
        at = pl.ds(pl.multiple_of(c * rows, rows), rows)
        for h in range(HG):
            q = qkv[at, h * head:(h + 1) * head]
            k = qkv[:, (HG + h) * head:(HG + h + 1) * head]
            v = qkv[:, (2 * HG + h) * head:(2 * HG + h + 1) * head]
            scores = lax.dot_general(q, k, (((1,), (1,)), ((), ())), preferred_element_type=f32)
            scores = scores * head ** (-0.5) + bias[at, :]
            exponent = jnp.exp(scores - jnp.max(scores, axis=-1, keepdims=True))
            total = jnp.sum(exponent, axis=-1, keepdims=True)
            value = jnp.dot(exponent.astype(jnp.bfloat16), v, preferred_element_type=f32)
            mixed[:, h * head:(h + 1) * head] = (value / total).astype(jnp.bfloat16)
        for g in range(F):
            outb[c, :, g * width:(g + 1) * width] = jnp.dot(
                mixed[...], wout[g], preferred_element_type=f32).astype(jnp.bfloat16)

    def s_copy(c, j, direction):
        device = p + 1 if direction == 0 else p - 1
        inbox = in_l if direction == 0 else in_r
        at = pl.ds(pl.multiple_of(j * PIECE, PIECE), PIECE)
        return pltpu.make_async_remote_copy(
            src_ref=outb.at[c, at, :], dst_ref=inbox.at[c, at, :],
            send_sem=rs.at[direction, c, j], recv_sem=rr.at[direction, c, j],
            device_id={"seq": device}, device_id_type=MESH)

    def y_copy(j):
        at = pl.ds(pl.multiple_of(j * PIECE, PIECE), PIECE)
        return pltpu.make_async_remote_copy(
            src_ref=fin.at[at, :], dst_ref=out_ref.at[at, :], send_sem=ys.at[j], recv_sem=yr.at[j],
            device_id={"segment": up}, device_id_type=MESH)

    def add_in(c, j, inbox):
        at = pl.ds(pl.multiple_of(j * PIECE, PIECE), PIECE)
        outb[c, at, :] = (outb[c, at, :].astype(f32) + inbox[c, at, :].astype(f32)).astype(jnp.bfloat16)

    def send_all(c, direction):
        def one(j, inner):
            s_copy(c, j, direction).start()
            return inner

        lax.fori_loop(0, pieces, one, 0)

    def share(e, carry):
        u = lax.div(e, 2)
        side = lax.rem(e, 2)
        own = u == Z - 1
        right = Z - 1 - u
        c = jnp.where(side == 0, jnp.where(own, p, right), u)
        valid = jnp.where(side == 0, jnp.logical_or(own, right > p), jnp.logical_and(jnp.logical_not(own), u < p))
        pl.when(valid)(lambda: partial(c))
        leaves = jnp.logical_and(valid, jnp.logical_not(own))
        pl.when(jnp.logical_and(leaves, jnp.logical_and(side == 0, p == 0)))(lambda: send_all(c, 0))
        pl.when(jnp.logical_and(leaves, jnp.logical_and(side == 1, p == Z - 1)))(lambda: send_all(c, 1))
        return carry

    lax.fori_loop(0, 2 * Z, share, 0)

    def relay(step, carry):
        r = step - p
        l = step - (Z - 1 - p)

        @pl.when(jnp.logical_and(p > 0, jnp.logical_and(r >= 0, r < (Z - 1 - p) * pieces)))
        def _():
            c, j = Z - 1 - lax.div(r, pieces), lax.rem(r, pieces)
            s_copy(c, j, 0).wait_recv()
            add_in(c, j, in_l)
            s_copy(c, j, 0).start()

        @pl.when(jnp.logical_and(p < Z - 1, jnp.logical_and(l >= 0, l < p * pieces)))
        def _():
            c, j = lax.div(l, pieces), lax.rem(l, pieces)
            s_copy(c, j, 1).wait_recv()
            add_in(c, j, in_r)
            s_copy(c, j, 1).start()
        return carry

    lax.fori_loop(0, (Z - 1) * pieces + Z, relay, 0)

    def finish(j, carry):
        at = pl.ds(pl.multiple_of(j * PIECE, PIECE), PIECE)
        acc[...] = outb[p, at, :].astype(f32)

        @pl.when(p < Z - 1)
        def _():
            s_copy(p, j, 1).wait_recv()
            acc[...] += in_r[p, at, :].astype(f32)

        @pl.when(p > 0)
        def _():
            s_copy(p, j, 0).wait_recv()
            acc[...] += in_l[p, at, :].astype(f32)
        fin[at, :] = (x_ref[at, :].astype(f32) + acc[...]).astype(jnp.bfloat16)
        y_copy(j).start()
        return carry

    lax.fori_loop(0, pieces, finish, 0)

    for slot in range(2 * X - 1):
        for k in range(PARTS):
            w_copy(f, k, sibling, slot).wait_send()
        for k in range(2):
            o_copy(f, k, sibling, slot).wait_send()

    def sent(j, carry):
        for t in range(Z - 1):
            @pl.when(jnp.logical_and(p < Z - 1, t <= p))
            def _():
                t_copy(p, j, 0, t).wait_send()

            @pl.when(jnp.logical_and(p > 0, t <= Z - 1 - p))
            def _():
                t_copy(p, j, 1, t).wait_send()
        for c in range(Z):
            pl.when(c > p)(lambda: s_copy(c, j, 0).wait_send())
            pl.when(c < p)(lambda: s_copy(c, j, 1).wait_send())
        y_copy(j).wait_send()
        y_copy(j).wait_recv()
        return carry

    lax.fori_loop(0, pieces, sent, 0)


def body(arriving, gain, input_weight, output_weight, block_pattern, S, F, Z):
    tokens = arriving[0, 0]
    rows, depth = tokens.shape
    slab, HG, triple, head = input_weight.shape[1:]
    columns = HG * triple * head
    width = output_weight.shape[-1]
    length = rows * Z
    pieces = rows // PIECE
    X = F // 2
    bf16 = jnp.bfloat16
    dma = pltpu.SemaphoreType.DMA
    vmem = pl.BlockSpec(memory_space=pltpu.VMEM)
    anywhere = pl.BlockSpec(memory_space=pl.ANY)
    passed = pl.pallas_call(
        functools.partial(kernel, S, F, Z, HG),
        out_shape=jax.ShapeDtypeStruct((rows, depth), bf16),
        in_specs=[vmem, vmem, pl.BlockSpec(memory_space=pltpu.HBM), pl.BlockSpec(memory_space=pltpu.HBM), pl.BlockSpec(memory_space=pltpu.SMEM)],
        out_specs=anywhere,
        scratch_shapes=[
            pltpu.VMEM((slab, triple, HG, head), bf16),
            pltpu.VMEM((length, depth), bf16),
            pltpu.VMEM((depth, columns), bf16),
            pltpu.VMEM((F, HG * head, width), bf16),
            pltpu.VMEM((length, columns), bf16),
            pltpu.VMEM((length, length), jnp.float32),
            pltpu.VMEM((Z, rows, depth), bf16),
            pltpu.VMEM((Z, rows, depth), bf16),
            pltpu.VMEM((Z, rows, depth), bf16),
            pltpu.VMEM((rows, HG * head), bf16),
            pltpu.VMEM((rows, depth), bf16),
            pltpu.VMEM((PIECE, depth), jnp.float32),
            dma((2,)),
            dma((2, Z - 1, pieces)),
            dma((2, Z - 1, pieces)),
            dma((2 * X - 1, PARTS)),
            dma((F, PARTS)),
            dma((2 * X - 1, 2)),
            dma((F, 2)),
            dma((2, Z, pieces)),
            dma((2, Z, pieces)),
            dma((pieces,)),
            dma((pieces,)),
        ],
        compiler_params=pltpu.CompilerParams(
            collective_id=0, has_side_effects=True, vmem_limit_bytes=48 * 1024 * 1024
        ),
    )(
        tokens,
        gain,
        jnp.swapaxes(input_weight[0], 1, 2),
        output_weight[0].reshape(HG * head, width),
        block_pattern[0, 0],
    )
    return passed[None, None]


def solution(mesh):
    in_specs = (
        P("segment", "fsdp", "seq", None),
        P("segment", None),
        P("segment", "fsdp", "seq", None, None),
        P("segment", "seq", None, "fsdp"),
        P("segment", "fsdp", None, None),
    )
    out_specs = P("segment", "fsdp", "seq", None)
    sizes = {"S": mesh.shape["segment"], "F": mesh.shape["fsdp"], "Z": mesh.shape["seq"]}
    return jax.shard_map(
        functools.partial(body, **sizes), mesh=mesh, in_specs=in_specs, out_specs=out_specs, check_vma=False
    )
```

```python
import functools

import jax
import jax.numpy as jnp
from jax import lax
from jax.experimental import pallas as pl
from jax.experimental.pallas import tpu as pltpu
from jax.sharding import PartitionSpec as P

BLOCK = 32
SEL = 6
PIECE = 32
STRIP = 32
PARTS = 4
EPSILON = 1e-05
MESH = pl.DeviceIdType.MESH


def kernel(
    S, F, Z, HG,
    x_hbm, gain_hbm, w_ref, o_ref, pat_ref, out_ref,
    x_ref, gain_ref, raw, tok, win, wout, qkv, bias, in_l, in_r, outb, mixed, fin, acc,
    local_sem, zs, zr, ws, wr, vs, vr, rs, rr, ys, yr,
):
    rows, depth = x_ref.shape
    length = rows * Z
    slab, head = w_ref.shape[0], w_ref.shape[3]
    columns = 3 * HG * head
    width = o_ref.shape[1]
    pieces = rows // PIECE
    part = slab // PARTS
    half = o_ref.shape[0] // 2
    X = F // 2
    f32 = jnp.float32

    s = lax.axis_index("segment")
    f = lax.axis_index("fsdp")
    p = lax.axis_index("seq")
    core = lax.rem(f, 2)
    chip = lax.div(f, 2)
    sibling = f + 1 - 2 * core
    up = lax.rem(s + 1, S)
    down = lax.rem(s + S - 1, S)

    own_w = pltpu.make_async_copy(w_ref, raw, local_sem.at[0])
    own_o = pltpu.make_async_copy(o_ref, wout.at[f], local_sem.at[1])
    own_x = pltpu.make_async_copy(x_hbm, x_ref, local_sem.at[2])
    own_gain = pltpu.make_async_copy(gain_hbm, gain_ref, local_sem.at[3])
    own_x.start()
    own_gain.start()
    own_w.start()
    own_o.start()

    barrier = pltpu.get_barrier_semaphore()

    def greet(device):
        pl.semaphore_signal(barrier, inc=1, device_id=device, device_id_type=MESH)

    pl.when(p > 0)(lambda: greet({"seq": p - 1}))
    pl.when(p < Z - 1)(lambda: greet({"seq": p + 1}))
    greet({"fsdp": sibling})
    for d in range(1, X):
        greet({"fsdp": lax.rem(chip + d, X) * 2 + core})
    greet({"segment": up})
    if S > 2:
        greet({"segment": down})
    always = 1 + (X - 1) + (2 if S > 2 else 1)
    pl.semaphore_wait(barrier, always + jnp.where(p > 0, 1, 0) + jnp.where(p < Z - 1, 1, 0))

    def w_rows(g, k):
        return win.at[pl.ds(pl.multiple_of(g * slab + k * part, part), part), :]

    def w_copy(g, k, device, slot):
        return pltpu.make_async_remote_copy(
            src_ref=w_rows(g, k), dst_ref=w_rows(g, k), send_sem=ws.at[slot, k], recv_sem=wr.at[g, k],
            device_id={"fsdp": device}, device_id_type=MESH)

    def o_copy(g, k, device, slot, own=False):
        at = pl.ds(k * half, half)
        return pltpu.make_async_remote_copy(
            src_ref=o_ref.at[at, :] if own else wout.at[g, at, :], dst_ref=wout.at[g, at, :],
            send_sem=vs.at[slot, k], recv_sem=vr.at[g, k],
            device_id={"fsdp": device}, device_id_type=MESH)

    def peer(d):
        return lax.rem(chip + d, X) * 2 + core

    def source(d):
        return lax.rem(chip + X - d, X) * 2 + core

    def send_o(k):
        for d in range(1, X):
            o_copy(f, k, peer(d), d - 1, True).start()
        o_copy(f, k, sibling, X - 1, True).start()

    def forward_o(k):
        for d in range(1, X):
            o_copy(source(d), k, sibling, X - 1 + d).wait_recv()
            o_copy(source(d), k, sibling, X - 1 + d).start()

    send_o(0)

    def t_rows(c, j):
        return tok.at[pl.ds(pl.multiple_of(c * rows + j * PIECE, PIECE), PIECE), :]

    def t_copy(c, j, direction, step):
        device = p + 1 if direction == 0 else p - 1
        return pltpu.make_async_remote_copy(
            src_ref=t_rows(c, j), dst_ref=t_rows(c, j),
            send_sem=zs.at[direction, step, j], recv_sem=zr.at[direction, step, j],
            device_id={"seq": device}, device_id_type=MESH)

    own_x.wait()
    own_gain.wait()

    def norm_piece(j, carry):
        values = x_ref[pl.ds(pl.multiple_of(j * PIECE, PIECE), PIECE), :].astype(f32)
        spread = jnp.mean(values * values, axis=-1, keepdims=True)
        t_rows(p, j)[...] = (values * lax.rsqrt(spread + EPSILON) * gain_ref[...]).astype(jnp.bfloat16)
        pl.when(p < Z - 1)(lambda: t_copy(p, j, 0, 0).start())
        pl.when(p > 0)(lambda: t_copy(p, j, 1, 0).start())
        return carry

    lax.fori_loop(0, pieces, norm_piece, 0)

    own_w.wait()

    def flatten(i, carry):
        flat = raw[pl.ds(i * STRIP, STRIP)].astype(f32).reshape(STRIP, columns)
        win[pl.ds(pl.multiple_of(f * slab + i * STRIP, STRIP), STRIP), :] = flat.astype(jnp.bfloat16)
        return carry

    for k in range(PARTS):
        lax.fori_loop(k * (part // STRIP), (k + 1) * (part // STRIP), flatten, 0)
        for d in range(1, X):
            w_copy(f, k, peer(d), d - 1).start()
        w_copy(f, k, sibling, X - 1).start()

    key_block = lax.broadcasted_iota(jnp.int32, (BLOCK, length), 1) // BLOCK

    def bias_rows(b, carry):
        hit = key_block == pat_ref[0, 0, b]
        for i in range(1, SEL):
            hit = jnp.logical_or(hit, key_block == pat_ref[i, 0, b])
        bias[pl.ds(pl.multiple_of(b * BLOCK, BLOCK), BLOCK), :] = jnp.where(hit, 0.0, -1e30)
        return carry

    lax.fori_loop(0, length // BLOCK, bias_rows, 0)

    def receive(t, forward):
        def one(j, carry):
            @pl.when(t < p)
            def _():
                t_copy(p - 1 - t, j, 0, t).wait_recv()
                if forward:
                    pl.when(p < Z - 1)(lambda: t_copy(p - 1 - t, j, 0, t + 1).start())

            @pl.when(t < Z - 1 - p)
            def _():
                t_copy(p + 1 + t, j, 1, t).wait_recv()
                if forward:
                    pl.when(p > 0)(lambda: t_copy(p + 1 + t, j, 1, t + 1).start())
            return carry

        lax.fori_loop(0, pieces, one, 0)

    def forward_w(k):
        for d in range(1, X):
            w_copy(source(d), k, sibling, X - 1 + d).wait_recv()
            w_copy(source(d), k, sibling, X - 1 + d).start()

    share_of = -(-PARTS // (Z - 2))
    for t in range(Z - 2):
        receive(t, True)
        for k in range(t * share_of, min(PARTS, (t + 1) * share_of)):
            forward_w(k)
    send_o(1)
    forward_o(0)
    for k in range(PARTS):
        for d in range(X):
            w_copy(lax.rem(chip + d, X) * 2 + 1 - core, k, sibling, 0).wait_recv()

    def project(e, carry):
        d = lax.div(e, 2)
        side = lax.rem(e, 2)

        @pl.when(e == 2 * Z - 2)
        def _():
            receive(Z - 2, False)
        c = jnp.where(side == 0, p - d, p + d)
        valid = jnp.where(side == 0, d <= p, jnp.logical_and(d >= 1, d <= Z - 1 - p))

        @pl.when(valid)
        def _():
            at = pl.ds(pl.multiple_of(c * rows, rows), rows)

            def one(h, inner):
                cols = pl.ds(pl.multiple_of(h * 3 * head, 3 * head), 3 * head)
                qkv[at, cols] = jnp.dot(
                    tok[at, :], win[:, cols], preferred_element_type=f32).astype(jnp.bfloat16)
                return inner

            lax.fori_loop(0, HG, one, 0)
        return carry

    lax.fori_loop(0, 2 * Z, project, 0)

    forward_o(1)
    own_o.wait()
    for k in range(2):
        for d in range(X):
            o_copy(lax.rem(chip + d, X) * 2 + 1 - core, k, sibling, 0).wait_recv()

    def partial(c):
        at = pl.ds(pl.multiple_of(c * rows, rows), rows)
        for h in range(HG):
            q = qkv[at, h * head:(h + 1) * head]
            k = qkv[:, (HG + h) * head:(HG + h + 1) * head]
            v = qkv[:, (2 * HG + h) * head:(2 * HG + h + 1) * head]
            scores = lax.dot_general(q, k, (((1,), (1,)), ((), ())), preferred_element_type=f32)
            scores = scores * head ** (-0.5) + bias[at, :]
            exponent = jnp.exp(scores - jnp.max(scores, axis=-1, keepdims=True))
            total = jnp.sum(exponent, axis=-1, keepdims=True)
            value = jnp.dot(exponent.astype(jnp.bfloat16), v, preferred_element_type=f32)
            mixed[:, h * head:(h + 1) * head] = (value / total).astype(jnp.bfloat16)
        for g in range(F):
            outb[c, :, g * width:(g + 1) * width] = jnp.dot(
                mixed[...], wout[g], preferred_element_type=f32).astype(jnp.bfloat16)

    def s_copy(c, j, direction):
        device = p + 1 if direction == 0 else p - 1
        inbox = in_l if direction == 0 else in_r
        at = pl.ds(pl.multiple_of(j * PIECE, PIECE), PIECE)
        return pltpu.make_async_remote_copy(
            src_ref=outb.at[c, at, :], dst_ref=inbox.at[c, at, :],
            send_sem=rs.at[direction, c, j], recv_sem=rr.at[direction, c, j],
            device_id={"seq": device}, device_id_type=MESH)

    def y_copy(j):
        at = pl.ds(pl.multiple_of(j * PIECE, PIECE), PIECE)
        return pltpu.make_async_remote_copy(
            src_ref=fin.at[at, :], dst_ref=out_ref.at[at, :], send_sem=ys.at[j], recv_sem=yr.at[j],
            device_id={"segment": up}, device_id_type=MESH)

    def add_in(c, j, inbox):
        at = pl.ds(pl.multiple_of(j * PIECE, PIECE), PIECE)
        outb[c, at, :] = (outb[c, at, :].astype(f32) + inbox[c, at, :].astype(f32)).astype(jnp.bfloat16)

    def send_all(c, direction):
        def one(j, inner):
            s_copy(c, j, direction).start()
            return inner

        lax.fori_loop(0, pieces, one, 0)

    def share(e, carry):
        u = lax.div(e, 2)
        side = lax.rem(e, 2)
        own = u == Z - 1
        right = Z - 1 - u
        c = jnp.where(side == 0, jnp.where(own, p, right), u)
        valid = jnp.where(side == 0, jnp.logical_or(own, right > p), jnp.logical_and(jnp.logical_not(own), u < p))
        pl.when(valid)(lambda: partial(c))
        leaves = jnp.logical_and(valid, jnp.logical_not(own))
        pl.when(jnp.logical_and(leaves, jnp.logical_and(side == 0, p == 0)))(lambda: send_all(c, 0))
        pl.when(jnp.logical_and(leaves, jnp.logical_and(side == 1, p == Z - 1)))(lambda: send_all(c, 1))
        return carry

    lax.fori_loop(0, 2 * Z, share, 0)

    def relay(step, carry):
        r = step - p
        l = step - (Z - 1 - p)

        @pl.when(jnp.logical_and(p > 0, jnp.logical_and(r >= 0, r < (Z - 1 - p) * pieces)))
        def _():
            c, j = Z - 1 - lax.div(r, pieces), lax.rem(r, pieces)
            s_copy(c, j, 0).wait_recv()
            add_in(c, j, in_l)
            s_copy(c, j, 0).start()

        @pl.when(jnp.logical_and(p < Z - 1, jnp.logical_and(l >= 0, l < p * pieces)))
        def _():
            c, j = lax.div(l, pieces), lax.rem(l, pieces)
            s_copy(c, j, 1).wait_recv()
            add_in(c, j, in_r)
            s_copy(c, j, 1).start()
        return carry

    lax.fori_loop(0, (Z - 1) * pieces + Z, relay, 0)

    def finish(j, carry):
        at = pl.ds(pl.multiple_of(j * PIECE, PIECE), PIECE)
        acc[...] = outb[p, at, :].astype(f32)

        @pl.when(p < Z - 1)
        def _():
            s_copy(p, j, 1).wait_recv()
            acc[...] += in_r[p, at, :].astype(f32)

        @pl.when(p > 0)
        def _():
            s_copy(p, j, 0).wait_recv()
            acc[...] += in_l[p, at, :].astype(f32)
        fin[at, :] = (x_ref[at, :].astype(f32) + acc[...]).astype(jnp.bfloat16)
        y_copy(j).start()
        return carry

    lax.fori_loop(0, pieces, finish, 0)

    for slot in range(2 * X - 1):
        for k in range(PARTS):
            w_copy(f, k, sibling, slot).wait_send()
        for k in range(2):
            o_copy(f, k, sibling, slot).wait_send()

    def sent(j, carry):
        for t in range(Z - 1):
            @pl.when(jnp.logical_and(p < Z - 1, t <= p))
            def _():
                t_copy(p, j, 0, t).wait_send()

            @pl.when(jnp.logical_and(p > 0, t <= Z - 1 - p))
            def _():
                t_copy(p, j, 1, t).wait_send()
        for c in range(Z):
            pl.when(c > p)(lambda: s_copy(c, j, 0).wait_send())
            pl.when(c < p)(lambda: s_copy(c, j, 1).wait_send())
        y_copy(j).wait_send()
        y_copy(j).wait_recv()
        return carry

    lax.fori_loop(0, pieces, sent, 0)


def body(arriving, gain, input_weight, output_weight, block_pattern, S, F, Z):
    tokens = arriving[0, 0]
    rows, depth = tokens.shape
    slab, HG, triple, head = input_weight.shape[1:]
    columns = HG * triple * head
    width = output_weight.shape[-1]
    length = rows * Z
    pieces = rows // PIECE
    X = F // 2
    bf16 = jnp.bfloat16
    dma = pltpu.SemaphoreType.DMA
    anywhere = pl.BlockSpec(memory_space=pl.ANY)
    passed = pl.pallas_call(
        functools.partial(kernel, S, F, Z, HG),
        out_shape=jax.ShapeDtypeStruct((rows, depth), bf16),
        in_specs=[anywhere, anywhere, anywhere, anywhere, pl.BlockSpec(memory_space=pltpu.SMEM)],
        out_specs=anywhere,
        scratch_shapes=[
            pltpu.VMEM((rows, depth), bf16),
            pltpu.VMEM((1, depth), jnp.float32),
            pltpu.VMEM((slab, triple, HG, head), bf16),
            pltpu.VMEM((length, depth), bf16),
            pltpu.VMEM((depth, columns), bf16),
            pltpu.VMEM((F, HG * head, width), bf16),
            pltpu.VMEM((length, columns), bf16),
            pltpu.VMEM((length, length), jnp.float32),
            pltpu.VMEM((Z, rows, depth), bf16),
            pltpu.VMEM((Z, rows, depth), bf16),
            pltpu.VMEM((Z, rows, depth), bf16),
            pltpu.VMEM((rows, HG * head), bf16),
            pltpu.VMEM((rows, depth), bf16),
            pltpu.VMEM((PIECE, depth), jnp.float32),
            dma((4,)),
            dma((2, Z - 1, pieces)),
            dma((2, Z - 1, pieces)),
            dma((2 * X - 1, PARTS)),
            dma((F, PARTS)),
            dma((2 * X - 1, 2)),
            dma((F, 2)),
            dma((2, Z, pieces)),
            dma((2, Z, pieces)),
            dma((pieces,)),
            dma((pieces,)),
        ],
        compiler_params=pltpu.CompilerParams(
            collective_id=0, has_side_effects=True, vmem_limit_bytes=63 * 1024 * 1024
        ),
    )(
        tokens,
        gain,
        jnp.swapaxes(input_weight[0], 1, 2),
        output_weight[0].reshape(HG * head, width),
        jnp.transpose(block_pattern[0], (2, 0, 1)),
    )
    return passed[None, None]


def solution(mesh):
    in_specs = (
        P("segment", "fsdp", "seq", None),
        P("segment", None),
        P("segment", "fsdp", "seq", None, None),
        P("segment", "seq", None, "fsdp"),
        P("segment", "fsdp", None, None),
    )
    out_specs = P("segment", "fsdp", "seq", None)
    sizes = {"S": mesh.shape["segment"], "F": mesh.shape["fsdp"], "Z": mesh.shape["seq"]}
    return jax.shard_map(
        functools.partial(body, **sizes), mesh=mesh, in_specs=in_specs, out_specs=out_specs, check_vma=False
    )
```

```python
import functools

import jax
import jax.numpy as jnp
from jax import lax
from jax.experimental import pallas as pl
from jax.experimental.pallas import tpu as pltpu
from jax.sharding import PartitionSpec as P

BLOCK = 32
SEL = 6
PIECE = 64
SUM = 32
STRIP = 32
PARTS = 4
EPSILON = 1e-05
MESH = pl.DeviceIdType.MESH


def kernel(
    S, F, Z, HG,
    x_hbm, gain_hbm, w_ref, o_ref, pat_ref, out_ref,
    x_ref, gain_ref, raw, tok, win, wout, qkv, bias, in_l, in_r, outb, mixed, fin, acc,
    local_sem, zs, zr, ws, wr, vs, vr, rs, rr, ys, yr,
):
    rows, depth = x_ref.shape
    length = rows * Z
    slab, head = w_ref.shape[0], w_ref.shape[3]
    columns = 3 * HG * head
    width = o_ref.shape[1]
    pieces = rows // PIECE
    sums = rows // SUM
    part = slab // PARTS
    half = o_ref.shape[0] // 2
    X = F // 2
    f32 = jnp.float32

    s = lax.axis_index("segment")
    f = lax.axis_index("fsdp")
    p = lax.axis_index("seq")
    core = lax.rem(f, 2)
    chip = lax.div(f, 2)
    sibling = f + 1 - 2 * core
    up = lax.rem(s + 1, S)
    down = lax.rem(s + S - 1, S)

    own_w = pltpu.make_async_copy(w_ref, raw, local_sem.at[0])
    own_o = pltpu.make_async_copy(o_ref, wout.at[f], local_sem.at[1])
    own_x = pltpu.make_async_copy(x_hbm, x_ref, local_sem.at[2])
    own_gain = pltpu.make_async_copy(gain_hbm, gain_ref, local_sem.at[3])
    own_x.start()
    own_gain.start()
    own_w.start()
    own_o.start()

    barrier = pltpu.get_barrier_semaphore()

    def greet(device):
        pl.semaphore_signal(barrier, inc=1, device_id=device, device_id_type=MESH)

    pl.when(p > 0)(lambda: greet({"seq": p - 1}))
    pl.when(p < Z - 1)(lambda: greet({"seq": p + 1}))
    greet({"fsdp": sibling})
    for d in range(1, X):
        greet({"fsdp": lax.rem(chip + d, X) * 2 + core})
    greet({"segment": up})
    if S > 2:
        greet({"segment": down})
    always = 1 + (X - 1) + (2 if S > 2 else 1)
    pl.semaphore_wait(barrier, always + jnp.where(p > 0, 1, 0) + jnp.where(p < Z - 1, 1, 0))

    def w_rows(g, k):
        return win.at[pl.ds(pl.multiple_of(g * slab + k * part, part), part), :]

    def w_copy(g, k, device, slot):
        return pltpu.make_async_remote_copy(
            src_ref=w_rows(g, k), dst_ref=w_rows(g, k), send_sem=ws.at[slot, k], recv_sem=wr.at[g, k],
            device_id={"fsdp": device}, device_id_type=MESH)

    def o_copy(g, k, device, slot, own=False):
        at = pl.ds(k * half, half)
        return pltpu.make_async_remote_copy(
            src_ref=o_ref.at[at, :] if own else wout.at[g, at, :], dst_ref=wout.at[g, at, :],
            send_sem=vs.at[slot, k], recv_sem=vr.at[g, k],
            device_id={"fsdp": device}, device_id_type=MESH)

    def peer(d):
        return lax.rem(chip + d, X) * 2 + core

    def source(d):
        return lax.rem(chip + X - d, X) * 2 + core

    def send_o(k):
        for d in range(1, X):
            o_copy(f, k, peer(d), d - 1, True).start()
        o_copy(f, k, sibling, X - 1, True).start()

    def forward_o(k):
        for d in range(1, X):
            o_copy(source(d), k, sibling, X - 1 + d).wait_recv()
            o_copy(source(d), k, sibling, X - 1 + d).start()

    send_o(0)

    def t_rows(c, j):
        return tok.at[pl.ds(pl.multiple_of(c * rows + j * PIECE, PIECE), PIECE), :]

    def t_copy(c, j, direction, step):
        device = p + 1 if direction == 0 else p - 1
        return pltpu.make_async_remote_copy(
            src_ref=t_rows(c, j), dst_ref=t_rows(c, j),
            send_sem=zs.at[direction, step, j], recv_sem=zr.at[direction, step, j],
            device_id={"seq": device}, device_id_type=MESH)

    own_x.wait()
    own_gain.wait()

    def norm_piece(j, carry):
        values = x_ref[pl.ds(pl.multiple_of(j * PIECE, PIECE), PIECE), :].astype(f32)
        spread = jnp.mean(values * values, axis=-1, keepdims=True)
        t_rows(p, j)[...] = (values * lax.rsqrt(spread + EPSILON) * gain_ref[...]).astype(jnp.bfloat16)
        pl.when(p < Z - 1)(lambda: t_copy(p, j, 0, 0).start())
        pl.when(p > 0)(lambda: t_copy(p, j, 1, 0).start())
        return carry

    lax.fori_loop(0, pieces, norm_piece, 0)

    own_w.wait()

    def flatten(i, carry):
        flat = raw[pl.ds(i * STRIP, STRIP)].astype(f32).reshape(STRIP, columns)
        win[pl.ds(pl.multiple_of(f * slab + i * STRIP, STRIP), STRIP), :] = flat.astype(jnp.bfloat16)
        return carry

    for k in range(PARTS):
        lax.fori_loop(k * (part // STRIP), (k + 1) * (part // STRIP), flatten, 0)
        for d in range(1, X):
            w_copy(f, k, peer(d), d - 1).start()
        w_copy(f, k, sibling, X - 1).start()

    key_block = lax.broadcasted_iota(jnp.int32, (BLOCK, length), 1) // BLOCK

    def bias_rows(b, carry):
        hit = key_block == pat_ref[0, 0, b]
        for i in range(1, SEL):
            hit = jnp.logical_or(hit, key_block == pat_ref[i, 0, b])
        bias[pl.ds(pl.multiple_of(b * BLOCK, BLOCK), BLOCK), :] = jnp.where(hit, 0.0, -1e30)
        return carry

    lax.fori_loop(0, length // BLOCK, bias_rows, 0)

    def receive(t, forward):
        def one(j, carry):
            @pl.when(t < p)
            def _():
                t_copy(p - 1 - t, j, 0, t).wait_recv()
                if forward:
                    pl.when(p < Z - 1)(lambda: t_copy(p - 1 - t, j, 0, t + 1).start())

            @pl.when(t < Z - 1 - p)
            def _():
                t_copy(p + 1 + t, j, 1, t).wait_recv()
                if forward:
                    pl.when(p > 0)(lambda: t_copy(p + 1 + t, j, 1, t + 1).start())
            return carry

        lax.fori_loop(0, pieces, one, 0)

    def forward_w(k):
        for d in range(1, X):
            w_copy(source(d), k, sibling, X - 1 + d).wait_recv()
            w_copy(source(d), k, sibling, X - 1 + d).start()

    share_of = -(-PARTS // (Z - 2))
    for t in range(Z - 2):
        receive(t, True)
        for k in range(t * share_of, min(PARTS, (t + 1) * share_of)):
            forward_w(k)
    send_o(1)
    forward_o(0)
    for k in range(PARTS):
        for d in range(X):
            w_copy(lax.rem(chip + d, X) * 2 + 1 - core, k, sibling, 0).wait_recv()

    def project(e, carry):
        d = lax.div(e, 2)
        side = lax.rem(e, 2)

        @pl.when(e == 2 * Z - 2)
        def _():
            receive(Z - 2, False)
        c = jnp.where(side == 0, p - d, p + d)
        valid = jnp.where(side == 0, d <= p, jnp.logical_and(d >= 1, d <= Z - 1 - p))

        @pl.when(valid)
        def _():
            at = pl.ds(pl.multiple_of(c * rows, rows), rows)

            def one(h, inner):
                cols = pl.ds(pl.multiple_of(h * 3 * head, 3 * head), 3 * head)
                qkv[at, cols] = jnp.dot(
                    tok[at, :], win[:, cols], preferred_element_type=f32).astype(jnp.bfloat16)
                return inner

            lax.fori_loop(0, HG, one, 0)
        return carry

    lax.fori_loop(0, 2 * Z, project, 0)

    forward_o(1)
    own_o.wait()
    for k in range(2):
        for d in range(X):
            o_copy(lax.rem(chip + d, X) * 2 + 1 - core, k, sibling, 0).wait_recv()

    def partial(c):
        at = pl.ds(pl.multiple_of(c * rows, rows), rows)
        for h in range(HG):
            q = qkv[at, h * head:(h + 1) * head]
            k = qkv[:, (HG + h) * head:(HG + h + 1) * head]
            v = qkv[:, (2 * HG + h) * head:(2 * HG + h + 1) * head]
            scores = lax.dot_general(q, k, (((1,), (1,)), ((), ())), preferred_element_type=f32)
            scores = scores * head ** (-0.5) + bias[at, :]
            exponent = jnp.exp(scores - jnp.max(scores, axis=-1, keepdims=True))
            total = jnp.sum(exponent, axis=-1, keepdims=True)
            value = jnp.dot(exponent.astype(jnp.bfloat16), v, preferred_element_type=f32)
            mixed[:, h * head:(h + 1) * head] = (value / total).astype(jnp.bfloat16)
        for g in range(F):
            outb[c, :, g * width:(g + 1) * width] = jnp.dot(
                mixed[...], wout[g], preferred_element_type=f32).astype(jnp.bfloat16)

    def s_copy(c, j, direction):
        device = p + 1 if direction == 0 else p - 1
        inbox = in_l if direction == 0 else in_r
        at = pl.ds(pl.multiple_of(j * SUM, SUM), SUM)
        return pltpu.make_async_remote_copy(
            src_ref=outb.at[c, at, :], dst_ref=inbox.at[c, at, :],
            send_sem=rs.at[direction, c, j], recv_sem=rr.at[direction, c, j],
            device_id={"seq": device}, device_id_type=MESH)

    def y_copy(j):
        at = pl.ds(pl.multiple_of(j * SUM, SUM), SUM)
        return pltpu.make_async_remote_copy(
            src_ref=fin.at[at, :], dst_ref=out_ref.at[at, :], send_sem=ys.at[j], recv_sem=yr.at[j],
            device_id={"segment": up}, device_id_type=MESH)

    def add_in(c, j, inbox):
        at = pl.ds(pl.multiple_of(j * SUM, SUM), SUM)
        outb[c, at, :] = (outb[c, at, :].astype(f32) + inbox[c, at, :].astype(f32)).astype(jnp.bfloat16)

    def send_all(c, direction):
        def one(j, inner):
            s_copy(c, j, direction).start()
            return inner

        lax.fori_loop(0, sums, one, 0)

    def share(e, carry):
        u = lax.div(e, 2)
        side = lax.rem(e, 2)
        own = u == Z - 1
        right = Z - 1 - u
        c = jnp.where(side == 0, jnp.where(own, p, right), u)
        valid = jnp.where(side == 0, jnp.logical_or(own, right > p), jnp.logical_and(jnp.logical_not(own), u < p))
        pl.when(valid)(lambda: partial(c))
        leaves = jnp.logical_and(valid, jnp.logical_not(own))
        pl.when(jnp.logical_and(leaves, jnp.logical_and(side == 0, p == 0)))(lambda: send_all(c, 0))
        pl.when(jnp.logical_and(leaves, jnp.logical_and(side == 1, p == Z - 1)))(lambda: send_all(c, 1))
        return carry

    lax.fori_loop(0, 2 * Z, share, 0)

    def relay(step, carry):
        r = step - p
        l = step - (Z - 1 - p)

        @pl.when(jnp.logical_and(p > 0, jnp.logical_and(r >= 0, r < (Z - 1 - p) * sums)))
        def _():
            c, j = Z - 1 - lax.div(r, sums), lax.rem(r, sums)
            s_copy(c, j, 0).wait_recv()
            add_in(c, j, in_l)
            s_copy(c, j, 0).start()

        @pl.when(jnp.logical_and(p < Z - 1, jnp.logical_and(l >= 0, l < p * sums)))
        def _():
            c, j = lax.div(l, sums), lax.rem(l, sums)
            s_copy(c, j, 1).wait_recv()
            add_in(c, j, in_r)
            s_copy(c, j, 1).start()
        return carry

    lax.fori_loop(0, (Z - 1) * sums + Z, relay, 0)

    def finish(j, carry):
        at = pl.ds(pl.multiple_of(j * SUM, SUM), SUM)
        acc[...] = outb[p, at, :].astype(f32)

        @pl.when(p < Z - 1)
        def _():
            s_copy(p, j, 1).wait_recv()
            acc[...] += in_r[p, at, :].astype(f32)

        @pl.when(p > 0)
        def _():
            s_copy(p, j, 0).wait_recv()
            acc[...] += in_l[p, at, :].astype(f32)
        fin[at, :] = (x_ref[at, :].astype(f32) + acc[...]).astype(jnp.bfloat16)
        y_copy(j).start()
        return carry

    lax.fori_loop(0, sums, finish, 0)

    for slot in range(2 * X - 1):
        for k in range(PARTS):
            w_copy(f, k, sibling, slot).wait_send()
        for k in range(2):
            o_copy(f, k, sibling, slot).wait_send()

    def sent(j, carry):
        for t in range(Z - 1):
            @pl.when(jnp.logical_and(p < Z - 1, t <= p))
            def _():
                t_copy(p, j, 0, t).wait_send()

            @pl.when(jnp.logical_and(p > 0, t <= Z - 1 - p))
            def _():
                t_copy(p, j, 1, t).wait_send()
        return carry

    lax.fori_loop(0, pieces, sent, 0)

    def sums_sent(j, carry):
        for c in range(Z):
            pl.when(c > p)(lambda: s_copy(c, j, 0).wait_send())
            pl.when(c < p)(lambda: s_copy(c, j, 1).wait_send())
        y_copy(j).wait_send()
        y_copy(j).wait_recv()
        return carry

    lax.fori_loop(0, sums, sums_sent, 0)


def body(arriving, gain, input_weight, output_weight, block_pattern, S, F, Z):
    tokens = arriving[0, 0]
    rows, depth = tokens.shape
    slab, HG, triple, head = input_weight.shape[1:]
    columns = HG * triple * head
    width = output_weight.shape[-1]
    length = rows * Z
    pieces = rows // PIECE
    sums = rows // SUM
    X = F // 2
    bf16 = jnp.bfloat16
    dma = pltpu.SemaphoreType.DMA
    anywhere = pl.BlockSpec(memory_space=pl.ANY)
    passed = pl.pallas_call(
        functools.partial(kernel, S, F, Z, HG),
        out_shape=jax.ShapeDtypeStruct((rows, depth), bf16),
        in_specs=[anywhere, anywhere, anywhere, anywhere, pl.BlockSpec(memory_space=pltpu.SMEM)],
        out_specs=anywhere,
        scratch_shapes=[
            pltpu.VMEM((rows, depth), bf16),
            pltpu.VMEM((1, depth), jnp.float32),
            pltpu.VMEM((slab, triple, HG, head), bf16),
            pltpu.VMEM((length, depth), bf16),
            pltpu.VMEM((depth, columns), bf16),
            pltpu.VMEM((F, HG * head, width), bf16),
            pltpu.VMEM((length, columns), bf16),
            pltpu.VMEM((length, length), jnp.float32),
            pltpu.VMEM((Z, rows, depth), bf16),
            pltpu.VMEM((Z, rows, depth), bf16),
            pltpu.VMEM((Z, rows, depth), bf16),
            pltpu.VMEM((rows, HG * head), bf16),
            pltpu.VMEM((rows, depth), bf16),
            pltpu.VMEM((SUM, depth), jnp.float32),
            dma((4,)),
            dma((2, Z - 1, pieces)),
            dma((2, Z - 1, pieces)),
            dma((2 * X - 1, PARTS)),
            dma((F, PARTS)),
            dma((2 * X - 1, 2)),
            dma((F, 2)),
            dma((2, Z, sums)),
            dma((2, Z, sums)),
            dma((sums,)),
            dma((sums,)),
        ],
        compiler_params=pltpu.CompilerParams(
            collective_id=0, has_side_effects=True, vmem_limit_bytes=63 * 1024 * 1024
        ),
    )(
        tokens,
        gain,
        jnp.swapaxes(input_weight[0], 1, 2),
        output_weight[0].reshape(HG * head, width),
        jnp.transpose(block_pattern[0], (2, 0, 1)),
    )
    return passed[None, None]


def solution(mesh):
    in_specs = (
        P("segment", "fsdp", "seq", None),
        P("segment", None),
        P("segment", "fsdp", "seq", None, None),
        P("segment", "seq", None, "fsdp"),
        P("segment", "fsdp", None, None),
    )
    out_specs = P("segment", "fsdp", "seq", None)
    sizes = {"S": mesh.shape["segment"], "F": mesh.shape["fsdp"], "Z": mesh.shape["seq"]}
    return jax.shard_map(
        functools.partial(body, **sizes), mesh=mesh, in_specs=in_specs, out_specs=out_specs, check_vma=False
    )
```
